32 devices in a mesh: rep: 2 (over y), expert: 16 (over z, x, core).
Axes of the slice: x: 2, y: 2, z: 4, core: 2. Of those that a mesh axis runs over, the one named last changes fastest.
Arguments:
- tokens: bfloat16 [2048, 4096], P('expert', 'rep')
- norm_gain: float32 [4096], P('rep'), may hold values from 0.25 to 1.75
- gate_weights: float32 [2048, 8], P('expert'), may hold values from 0.1 to 0.6
- exit_flags: int32 [2048], P('expert'), may hold values from 0 to 1, as said below
- routes: int32 [2048, 8], P('expert'), may hold values from 0 to 31, as said below
- next_device: int32 [2048], P('expert'), may hold values from 0 to 15, as said below
- up_weight: bfloat16 [32, 4096, 1024], P('expert', 'rep'), may hold values from -0.09375 to 0.09375
- down_weight: bfloat16 [32, 1024, 4096], P('expert', None, 'rep'), may hold values from -0.1875 to 0.1875
Outputs:
- handed: float32 [1024, 4096], P('expert', 'rep')
The draws below stay inside these ranges and needn't reach their ends.
Inputs may be any that keep to these rules, and one draw needn't show every extreme that they name: `exit_flags`: one block of 128 rows holds at most 64 live rows; some block holds exactly 64. `routes`: each row names 8 different experts. Among the live rows of one block, every expert is named the same number of times up to one, so at most 16 times; a block with 64 live rows names every expert exactly 16 times. `next_device`: among the live rows of one block, every value is named the same number of times up to one, so at most 4 times.
All inputs are finite; a program needn't handle non-finite values.
Results may differ from the reference program's by a relative error of at most 0.0017.
Values may be sent and summed in bfloat16 or wider, within the bound.
A program may use at most 64 MiB of HBM per device.

```python
import jax
import jax.numpy as jnp
from jax import lax

D = 4096
HID = 1024
TOP = 8
ROW_DEV = 128
EXPERTS = 32
ROWS = 2048
MAX_SURVIVE_ROWS = 64
CAP = 16
HCAP = 4
HANDED = 1024
N_EXPERT = 16


def plan_rows(key):
    block_list = ROWS // ROW_DEV
    keys = jax.random.split(jax.random.fold_in(key, 71), 5)
    depth_level = jax.random.randint(keys[0], (block_list,), 0, 4)
    surviving_rows = MAX_SURVIVE_ROWS // 8 * jnp.left_shift(1, depth_level)
    forced_exit = jax.random.randint(keys[1], (), 0, block_list)
    surviving_rows = jnp.where(jnp.arange(block_list) == forced_exit, MAX_SURVIVE_ROWS, surviving_rows)
    sorted_order = jax.vmap(lambda single: jax.random.permutation(single, ROW_DEV))(jax.random.split(keys[2], block_list))
    alive_mask = (sorted_order < surviving_rows[:, None]).astype(jnp.int32)
    live_rank = jnp.cumsum(alive_mask, axis=1) - alive_mask
    dead_rank = jnp.cumsum(1 - alive_mask, axis=1) - (1 - alive_mask)
    return (alive_mask, live_rank, dead_rank, keys[3], keys[4])


def draw_exit_flags(key, part):
    alive_mask, live_rank, dead_rank, key_route, key_dest = plan_rows(key)
    return (1 - alive_mask).reshape(ROWS).astype(jnp.int32)


def draw_routes(key, part):
    alive_mask, live_rank, dead_rank, key_route, key_dest = plan_rows(key)
    block_list = ROWS // ROW_DEV
    perms = jax.vmap(lambda single: jax.random.permutation(single, EXPERTS))(jax.random.split(key_route, block_list * CAP))
    perms = perms.reshape(block_list, CAP, EXPERTS)
    slot_k = jnp.arange(TOP)[None, None, :]
    live_pair = live_rank[:, :, None] * TOP + slot_k
    dead_pair = dead_rank[:, :, None] * TOP + slot_k
    alive_b = alive_mask[:, :, None] > 0
    round_idx = jnp.where(alive_b, live_pair // EXPERTS, 0)
    column = jnp.where(alive_b, live_pair % EXPERTS, dead_pair % EXPERTS)
    block_idx = jnp.broadcast_to(jnp.arange(block_list)[:, None, None], column.shape)
    chosen = perms[block_idx, round_idx, column]
    return chosen.reshape(ROWS, TOP).astype(jnp.int32)


def draw_next_device(key, part):
    alive_mask, live_rank, dead_rank, key_route, key_dest = plan_rows(key)
    block_list = ROWS // ROW_DEV
    perms = jax.vmap(lambda single: jax.random.permutation(single, N_EXPERT))(jax.random.split(key_dest, block_list))
    index = jnp.where(alive_mask > 0, live_rank, dead_rank) % N_EXPERT
    block_idx = jnp.broadcast_to(jnp.arange(block_list)[:, None], index.shape)
    return perms[block_idx, index].reshape(ROWS).astype(jnp.int32)


def draw_tokens(key, part):
    keys = jax.random.split(jax.random.fold_in(key, 5), 4)
    column_pos = jnp.arange(D, dtype=jnp.float32) / D
    column_scale = 10.0 ** (jax.random.uniform(keys[0], (D,)) - 0.5) * 3.0 ** (0.6 * column_pos - 0.3)
    row_scale = 10.0 ** (jax.random.uniform(keys[1], (ROWS,)) - 0.5)
    base = jnp.clip(jax.random.normal(keys[3], (ROWS, D)), -4.0, 4.0)
    values = row_scale[:, None] * column_scale[None, :] * base
    return values.astype(jnp.float32).astype(jnp.bfloat16)


def shard_levels(stream_key, dims, shards, smallest, top_value):
    def one(dim, parts):
        heights = jax.random.uniform(jax.random.fold_in(jax.random.fold_in(stream_key, 6), dim), (parts,), jnp.float32, smallest / len(shards), top_value / len(shards))
        return jnp.repeat(jnp.exp(heights), dims[dim] // parts).reshape((-1,) + (1,) * (len(dims) - dim - 1))

    level = one(*shards[0])
    for cut in shards[1:]:
        level = level * one(*cut)
    return level


def noise(rng, shape, scale, reach, cuts=(), kind=jnp.bfloat16):
    array = scale * jax.random.normal(rng, shape, jnp.float32)
    if cuts:
        array = array * shard_levels(rng, shape, cuts, -0.22, 0.18)
    return jnp.clip(array, -reach, reach).astype(kind)


def setup_inputs(seed: int = 0) -> dict:
    splits = jax.random.split(jax.random.key(seed), 9)
    return {
        "tokens": draw_tokens(jax.random.fold_in(splits[8], 71), 0),
        "norm_gain": jnp.clip(1.0 + 0.15 * jax.random.normal(splits[1], (D,), jnp.float32), 0.25, 1.75),
        "gate_weights": jnp.clip(0.1 + 0.5 * jax.random.uniform(splits[2], (ROWS, TOP), jnp.float32) ** shard_levels(splits[2], (ROWS, TOP), ((0, 16),), -0.2, 0.2), 0.1, 0.6),
        "exit_flags": draw_exit_flags(jax.random.fold_in(splits[8], 71), 0),
        "routes": draw_routes(jax.random.fold_in(splits[8], 71), 0),
        "next_device": draw_next_device(jax.random.fold_in(splits[8], 71), 0),
        "up_weight": noise(splits[6], (EXPERTS, D, HID), D ** -0.5, 0.09375, ((0, 16), (1, 2))),
        "down_weight": noise(splits[7], (EXPERTS, HID, D), HID ** -0.5, 0.1875, ((0, 16), (2, 2))),
    }


def reference(tokens, norm_gain, gate_weights, exit_flags, routes, next_device, up_weight, down_weight):
    widened = tokens.astype(jnp.float32)
    rinv_rows = lax.rsqrt(lax.optimization_barrier(jnp.sum(widened * widened, axis=1)) / D + 1e-06)
    normed = (widened * rinv_rows[:, None] * norm_gain[None, :]).astype(jnp.bfloat16)
    survive = (1 - exit_flags).astype(jnp.int32)
    pair_live = jnp.repeat(survive, TOP)
    route_flat = routes.reshape(-1).astype(jnp.int32)
    one_hot = (route_flat[:, None] == jnp.arange(EXPERTS, dtype=jnp.int32)[None, :]).astype(jnp.int32) * pair_live[:, None]
    blocked = one_hot.reshape(N_EXPERT, ROW_DEV * TOP, EXPERTS)
    earlier = (jnp.cumsum(blocked, axis=1) - blocked).reshape(ROWS * TOP, EXPERTS)
    position = lax.optimization_barrier(jnp.sum(earlier * one_hot, axis=1)).astype(jnp.int32)
    source_dev = jnp.arange(ROWS * TOP, dtype=jnp.int32) // (ROW_DEV * TOP)
    slot_index = jnp.where(pair_live > 0, source_dev * CAP + position, N_EXPERT * CAP).astype(jnp.int32)
    row_plus = (jnp.arange(ROWS * TOP, dtype=jnp.int32) // TOP + 1).astype(jnp.int32)
    table = jnp.zeros((EXPERTS, N_EXPERT * CAP), jnp.int32).at[route_flat, slot_index].set(row_plus, mode='drop')
    padded = jnp.concatenate([jnp.zeros((1, D), jnp.bfloat16), normed], axis=0)

    def per_expert(items):
        w_up, w_down, row_ids = items
        gathered = padded[row_ids]
        hidden = jnp.dot(gathered, w_up, preferred_element_type=jnp.float32)
        activated = jax.nn.silu(hidden).astype(jnp.bfloat16)
        return jnp.dot(activated, w_down, preferred_element_type=jnp.float32).astype(jnp.bfloat16)
    expert_out = lax.map(per_expert, (up_weight, down_weight, table)).reshape(EXPERTS * N_EXPERT * CAP, D)
    chosen = (route_flat * (N_EXPERT * CAP) + jnp.minimum(slot_index, N_EXPERT * CAP - 1)).reshape(ROWS, TOP)
    mixture = jnp.zeros((ROWS, D), jnp.float32)
    for slot_k in range(TOP):
        mixture = mixture + gate_weights[:, slot_k:slot_k + 1] * expert_out[chosen[:, slot_k]].astype(jnp.float32)
    updated = widened + mixture
    dest_hot = (next_device[:, None] == jnp.arange(N_EXPERT, dtype=jnp.int32)[None, :]).astype(jnp.int32) * survive[:, None]
    dest_block = dest_hot.reshape(N_EXPERT, ROW_DEV, N_EXPERT)
    dest_before = (jnp.cumsum(dest_block, axis=1) - dest_block).reshape(ROWS, N_EXPERT)
    handoff_pos = lax.optimization_barrier(jnp.sum(dest_before * dest_hot, axis=1)).astype(jnp.int32)
    source_row_dev = jnp.arange(ROWS, dtype=jnp.int32) // ROW_DEV
    target = next_device * (N_EXPERT * HCAP) + source_row_dev * HCAP + handoff_pos
    target = jnp.where(survive > 0, target, HANDED).astype(jnp.int32)
    return jnp.zeros((HANDED, D), jnp.float32).at[target].set(updated, mode='drop')
```

```python
import jax
import jax.numpy as jnp
from jax import lax
from jax.sharding import PartitionSpec as P

F32 = jnp.float32
BF16 = jnp.bfloat16


def lower_ones(n):
    i = jnp.arange(n)
    return (i[:, None] > i[None, :]).astype(BF16)


def per_device(
    tokens, norm_gain, gate_weights, exit_flags, routes, next_device, up_weight, down_weight
):
    row_count, width = tokens.shape
    owners = lax.axis_size("expert")
    reps = lax.axis_size("rep")
    local_experts = up_weight.shape[0]
    top = routes.shape[1]
    experts_all = local_experts * owners
    most_live = row_count // 2
    cap = top * most_live // experts_all
    hand_cap = (most_live + owners - 1) // owners
    packed_rows = owners * hand_cap

    live = exit_flags == 0
    dest_hot = (
        (next_device[:, None] == jnp.arange(owners)[None, :]) & live[:, None]
    ).astype(BF16)
    before = jnp.dot(lower_ones(row_count), dest_hot, preferred_element_type=F32)
    pos = jnp.sum(before * dest_hot.astype(F32), axis=1).astype(jnp.int32)
    slot = jnp.where(live, next_device * hand_cap + pos, packed_rows)
    pick = slot[None, :] == jnp.arange(packed_rows)[:, None]
    packed = jnp.dot(pick.astype(BF16), tokens, preferred_element_type=F32)
    square = jnp.sum(packed * packed, axis=1)
    dense_gate = jnp.sum(
        jnp.where(
            routes[:, :, None] == jnp.arange(experts_all)[None, None, :],
            gate_weights[:, :, None],
            0.0,
        ),
        axis=1,
    )
    gate_packed = jnp.sum(
        jnp.where(pick[:, :, None], dense_gate[None, :, :], 0.0), axis=1
    )
    aux = jnp.concatenate([gate_packed, square[:, None]], axis=1)

    rows = lax.all_gather(packed.astype(BF16), "expert")
    aux = lax.all_gather(aux, "expert")
    rinv = lax.rsqrt(lax.psum(aux[:, :, experts_all], "rep") / (width * reps) + 1e-06)

    me = lax.axis_index("expert")
    gates = lax.dynamic_slice_in_dim(aux, me * local_experts, local_experts, axis=2)
    routed = (gates > 0).astype(BF16)
    place = jnp.einsum(
        "rt,ite->ire", lower_ones(packed_rows), routed, preferred_element_type=F32
    ).astype(jnp.int32)
    hot = (place[:, :, :, None] == jnp.arange(cap)) & (routed > 0)[:, :, :, None]
    hot = hot.reshape(owners, packed_rows, local_experts * cap)
    slots = jnp.einsum("irs,ird->isd", hot.astype(BF16), rows, preferred_element_type=F32)
    rinv_slot = jnp.sum(jnp.where(hot, rinv[:, :, None], 0.0), axis=1)
    normed = (slots * rinv_slot[:, :, None] * norm_gain).astype(BF16)
    normed = normed.reshape(owners, local_experts, cap, width)

    hidden = jnp.einsum("iecd,edh->eich", normed, up_weight, preferred_element_type=F32)
    hidden = lax.psum(hidden, "rep")
    act = jax.nn.silu(hidden).astype(BF16)
    out = jnp.einsum("eich,ehd->iecd", act, down_weight, preferred_element_type=F32)
    out = out.astype(BF16).reshape(owners, local_experts * cap, width)

    gate_slot = jnp.where(
        hot, jnp.repeat(gates, cap, axis=2), 0.0
    )
    high = gate_slot.astype(BF16)
    low = (gate_slot - high.astype(F32)).astype(BF16)
    mix = jnp.einsum(
        "irs,isd->ird",
        jnp.concatenate([high, low], axis=2),
        jnp.concatenate([out, out], axis=1),
        preferred_element_type=F32,
    )
    mix = mix.reshape(owners, owners, hand_cap, width).swapaxes(0, 1)
    summed = lax.psum_scatter(mix.astype(REDUCE), "expert", scatter_dimension=0, tiled=False)
    own = lax.dynamic_slice_in_dim(
        rows.reshape(owners, owners, hand_cap, width), me, 1, axis=1
    )[:, 0]
    return (own.astype(F32) + summed.astype(F32)).reshape(owners * hand_cap, width)


REDUCE = BF16


def solution(mesh):
    in_specs = (
        P("expert", "rep"),
        P("rep"),
        P("expert", None),
        P("expert"),
        P("expert", None),
        P("expert"),
        P("expert", "rep", None),
        P("expert", None, "rep"),
    )
    return jax.shard_map(
        per_device, mesh=mesh, in_specs=in_specs, out_specs=P("expert", "rep"), check_vma=False
    )
```

```python
import jax
import jax.numpy as jnp
from jax import lax
from jax.sharding import PartitionSpec as P

F32 = jnp.float32
BF16 = jnp.bfloat16


def lower_ones(n):
    i = jnp.arange(n)
    return (i[:, None] > i[None, :]).astype(BF16)


def rep_sum(value, reps):
    if reps != 2:
        return lax.psum(value, "rep")
    return value + lax.ppermute(value.astype(BF16), "rep", [(0, 1), (1, 0)]).astype(F32)


def expert_reduce(value):
    return lax.psum_scatter(value, "expert", scatter_dimension=0, tiled=False)


def per_device(
    tokens, norm_gain, gate_weights, exit_flags, routes, next_device, up_weight, down_weight
):
    row_count, width = tokens.shape
    owners = lax.axis_size("expert")
    reps = lax.axis_size("rep")
    local_experts = up_weight.shape[0]
    top = routes.shape[1]
    experts_all = local_experts * owners
    most_live = row_count // 2
    cap = top * most_live // experts_all
    hand_cap = (most_live + owners - 1) // owners
    packed_rows = owners * hand_cap

    live = exit_flags == 0
    dest_hot = (
        (next_device[:, None] == jnp.arange(owners)[None, :]) & live[:, None]
    ).astype(BF16)
    before = jnp.dot(lower_ones(row_count), dest_hot, preferred_element_type=F32)
    pos = jnp.sum(before * dest_hot.astype(F32), axis=1).astype(jnp.int32)
    slot = jnp.where(live, next_device * hand_cap + pos, packed_rows)
    pick = slot[None, :] == jnp.arange(packed_rows)[:, None]
    packed = jnp.dot(pick.astype(BF16), tokens, preferred_element_type=F32)
    square = jnp.sum(packed * packed, axis=1)
    dense_gate = jnp.sum(
        jnp.where(
            routes[:, :, None] == jnp.arange(experts_all)[None, None, :],
            gate_weights[:, :, None],
            0.0,
        ),
        axis=1,
    )
    gate_packed = jnp.sum(
        jnp.where(pick[:, :, None], dense_gate[None, :, :], 0.0), axis=1
    )
    aux = jnp.concatenate([gate_packed, square[:, None]], axis=1)

    pieces = []
    rest = aux
    for _ in range(3):
        piece = lax.reduce_precision(rest, 8, 7)
        pieces.append(piece.astype(BF16))
        rest = rest - piece
    side = jnp.concatenate(pieces, axis=1)
    side = jnp.pad(side, ((0, 0), (0, -side.shape[1] % 128)))
    both = lax.all_gather(jnp.concatenate([packed.astype(BF16), side], axis=1), "expert")
    rows = both[:, :, :width]
    parts = both[:, :, width : width + 3 * aux.shape[1]].astype(F32)
    parts = parts.reshape(owners, packed_rows, 3, aux.shape[1])
    aux = parts[:, :, 0] + parts[:, :, 1] + parts[:, :, 2]
    rinv = lax.rsqrt(lax.psum(aux[:, :, experts_all], "rep") / (width * reps) + 1e-06)

    me = lax.axis_index("expert")
    gates = lax.dynamic_slice_in_dim(aux, me * local_experts, local_experts, axis=2)
    routed = (gates > 0).astype(BF16)
    place = jnp.einsum(
        "rt,ite->ire", lower_ones(packed_rows), routed, preferred_element_type=F32
    ).astype(jnp.int32)
    hot = (place[:, :, :, None] == jnp.arange(cap)) & (routed > 0)[:, :, :, None]
    hot = hot.reshape(owners, packed_rows, local_experts * cap)
    slots = jnp.einsum("irs,ird->isd", hot.astype(BF16), rows, preferred_element_type=F32)
    rinv_slot = jnp.sum(jnp.where(hot, rinv[:, :, None], 0.0), axis=1)
    normed = (slots * rinv_slot[:, :, None] * norm_gain).astype(BF16)
    normed = normed.reshape(owners, local_experts, cap, width)

    outs = []
    sums = []
    for e in range(local_experts):
        flat = normed[:, e].reshape(owners * cap, width)
        sums.append(
            rep_sum(jnp.dot(flat, up_weight[e], preferred_element_type=F32), reps)
        )
    for e in range(local_experts):
        act = jax.nn.silu(sums[e]).astype(BF16)
        out = jnp.dot(act, down_weight[e], preferred_element_type=F32).astype(BF16)
        outs.append(out.reshape(owners, cap, width))
    out = jnp.stack(outs, axis=1)
    out = out.reshape(owners * local_experts * cap, width)

    gate_slot = jnp.where(hot, jnp.repeat(gates, cap, axis=2), 0.0).astype(BF16)
    gate_slot = gate_slot.reshape(owners, owners, hand_cap, -1).transpose(1, 0, 2, 3)
    same = jnp.arange(owners)[:, None] == jnp.arange(owners)[None, :]
    weights = jnp.where(same[None, :, None, :, None], gate_slot[:, :, :, None, :], 0)
    weights = weights.reshape(owners * packed_rows, -1)
    mix = jnp.dot(weights, out, preferred_element_type=F32).astype(BF16)
    summed = expert_reduce(mix.reshape(owners, packed_rows, width))
    own = lax.dynamic_slice_in_dim(
        rows.reshape(owners, owners, hand_cap, width), me, 1, axis=1
    )[:, 0]
    return own.reshape(packed_rows, width).astype(F32) + summed.astype(F32)


def solution(mesh):
    in_specs = (
        P("expert", "rep"),
        P("rep"),
        P("expert", None),
        P("expert"),
        P("expert", None),
        P("expert"),
        P("expert", "rep", None),
        P("expert", None, "rep"),
    )
    return jax.shard_map(
        per_device, mesh=mesh, in_specs=in_specs, out_specs=P("expert", "rep"), check_vma=False
    )
```

```python
import functools

import jax
import jax.numpy as jnp
from jax import lax
from jax.experimental import pallas as pl
from jax.experimental.pallas import tpu as pltpu
from jax.sharding import PartitionSpec as P

F32 = jnp.float32
BF16 = jnp.bfloat16


def lower_ones(n):
    i = jnp.arange(n)
    return (i[:, None] > i[None, :]).astype(BF16)


def rep_sum(value, reps):
    if reps != 2:
        return lax.psum(value, "rep")
    return value + lax.ppermute(value.astype(BF16), "rep", [(0, 1), (1, 0)]).astype(F32)


Z, X, C = 4, 2, 2
MESH = pl.DeviceIdType.MESH


def place_of():
    me = lax.axis_index("expert")
    return lax.axis_index("rep"), me // (X * C), me // C % X, me % C


def index_of(z, x, c):
    return (z * X + x) * C + c


def greet(rep, z, x, c):
    barrier = pltpu.get_barrier_semaphore()

    def signal(where):
        pl.semaphore_signal(barrier, inc=1, device_id=(rep, where), device_id_type=MESH)

    signal(index_of(z, 1 - x, c))
    signal(index_of(z, x, 1 - c))
    pl.when(z > 0)(lambda: signal(index_of(z - 1, x, c)))
    pl.when(z < Z - 1)(lambda: signal(index_of(z + 1, x, c)))
    inner = (z > 0) & (z < Z - 1)
    pl.when(inner)(lambda: pl.semaphore_wait(barrier, 4))
    pl.when(jnp.logical_not(inner))(lambda: pl.semaphore_wait(barrier, 3))


def gather_kernel(own, out, local_sem, send, recv):
    rep, z, x, c = place_of()
    mine = index_of(z, x, c)
    greet(rep, z, x, c)
    local = pltpu.make_async_copy(own, out.at[mine], local_sem)
    local.start()

    def copy(block, sem, where, source=None):
        return pltpu.make_async_remote_copy(
            src_ref=out.at[block] if source is None else source,
            dst_ref=out.at[block],
            send_sem=send.at[sem],
            recv_sem=recv.at[block],
            device_id=(rep, where),
            device_id_type=MESH,
        )

    def forward(act):
        for d in range(Z):
            for sign in (1, -1):
                if d == 0 and sign < 0:
                    continue
                src = z - sign * d
                ok = (src >= 0) & (src < Z)

                def step(d=d, sign=sign, src=src):
                    block = index_of(src, x, c)
                    source = own if d == 0 else None
                    if d > 0:
                        act.wait(copy(block, 0, mine))
                    if d == 0 or sign > 0:
                        pl.when(z < Z - 1)(
                            lambda: act(copy(block, d, index_of(z + 1, x, c), source))
                        )
                    if d == 0 or sign < 0:
                        pl.when(z > 0)(
                            lambda: act(copy(block, 4 + d, index_of(z - 1, x, c), source))
                        )
                    act(copy(block, 8 + src, index_of(z, 1 - x, c), source))
                    act(copy(block, 12 + src, index_of(z, x, 1 - c), source))

                if d == 0:
                    step()
                else:
                    pl.when(ok)(step)
        for d in range(Z):
            for sign in (1, -1):
                if d == 0 and sign < 0:
                    continue
                src = z - sign * d

                def step(src=src):
                    block = index_of(src, 1 - x, c)
                    act.wait(copy(block, 0, mine))
                    act(copy(block, 16 + src, index_of(z, x, 1 - c)))

                pl.when((src >= 0) & (src < Z))(step)

    class Start:
        def __call__(self, op):
            op.start()

        def wait(self, op):
            op.wait_recv()

    class Finish:
        def __call__(self, op):
            op.wait_send()

        def wait(self, op):
            pass

    forward(Start())
    for a in range(Z):
        for b in range(X):
            copy(index_of(a, b, 1 - c), 0, mine).wait_recv()
    forward(Finish())
    local.wait()


def expert_gather(value):
    if (lax.axis_size("rep"), lax.axis_size("expert")) != (2, Z * X * C):
        return lax.all_gather(value, "expert")
    n = Z * X * C
    return pl.pallas_call(
        gather_kernel,
        out_shape=jax.ShapeDtypeStruct((n,) + value.shape, value.dtype),
        in_specs=[pl.BlockSpec(memory_space=pltpu.VMEM)],
        out_specs=pl.BlockSpec(memory_space=pltpu.VMEM),
        scratch_shapes=[
            pltpu.SemaphoreType.DMA,
            pltpu.SemaphoreType.DMA((20,)),
            pltpu.SemaphoreType.DMA((n,)),
        ],
        compiler_params=pltpu.CompilerParams(
            collective_id=0, has_side_effects=True, vmem_limit_bytes=24 << 20
        ),
    )(value)


def reduce_kernel(value, out, acc, from_c, from_x, part, from_z, send, recv):
    rep, z, x, c = place_of()
    greet(rep, z, x, c)

    def copy(source, target, sem, z2, x2, c2):
        return pltpu.make_async_remote_copy(
            src_ref=source,
            dst_ref=target,
            send_sem=send.at[sem],
            recv_sem=recv.at[sem],
            device_id=(rep, index_of(z2, x2, c2)),
            device_id_type=MESH,
        )

    order = (Z - 1, 0, 1, 2)

    def to_c(a, far):
        b = 1 - x if far else x
        k = (0 if far else Z) + a
        return copy(value.at[index_of(a, b, 1 - c)], from_c.at[k], k, z, x, 1 - c)

    def to_x(a):
        return copy(acc.at[a], from_x.at[a], 8 + a, z, 1 - x, c)

    def to_z(a, way):
        k = way * Z + a
        return copy(part.at[k], from_z.at[k], 12 + k, z + 1 - 2 * way, x, c)

    def arrived(a, way):
        k = way * Z + a
        copy(part.at[k], from_z.at[k], 12 + k, z, x, 1 - c).wait_recv()

    def wide(ref):
        return ref.astype(F32)

    for far in (True, False):
        for a in order:
            to_c(a, far).start()
    for a in order:
        to_c(a, True).wait_recv()
        acc[a] = (wide(value[index_of(a, 1 - x, c)]) + wide(from_c[a])).astype(BF16)
        to_x(a).start()
    for a in order:
        to_c(a, False).wait_recv()
        acc[Z + a] = (wide(value[index_of(a, x, c)]) + wide(from_c[Z + a])).astype(BF16)
    for a in order:
        to_x(a).wait_recv()
        acc[Z + a] = (wide(acc[Z + a]) + wide(from_x[a])).astype(BF16)

        def first(way, a=a):
            part[way * Z + a] = acc[Z + a]
            to_z(a, way).start()

        pl.when((z == 0) & (a > z))(functools.partial(first, 0))
        pl.when((z == Z - 1) & (a < z))(functools.partial(first, 1))

    def on(way, a):
        k = way * Z + a
        arrived(a, way)
        part[k] = (wide(acc[Z + a]) + wide(from_z[k])).astype(BF16)
        to_z(a, way).start()

    for a in range(Z):
        far = Z - 1 - a
        pl.when((z > 0) & (far > z))(functools.partial(on, 0, far))
        pl.when((z < Z - 1) & (a < z))(functools.partial(on, 1, a))
    out[...] = wide(acc[Z + z])

    def last(way):
        arrived(z, way)
        out[...] += wide(from_z[way * Z + z])

    pl.when(z > 0)(functools.partial(last, 0))
    pl.when(z < Z - 1)(functools.partial(last, 1))
    for a in range(Z):
        to_c(a, True).wait_send()
        to_c(a, False).wait_send()
        to_x(a).wait_send()
        pl.when(a > z)(lambda a=a: to_z(a, 0).wait_send())
        pl.when(a < z)(lambda a=a: to_z(a, 1).wait_send())


def expert_reduce(value):
    n, rows, width = value.shape
    if (lax.axis_size("rep"), n) != (2, Z * X * C):
        return lax.psum_scatter(value, "expert", scatter_dimension=0, tiled=False)
    blocks = [pltpu.VMEM((k, rows, width), BF16) for k in (8, 8, 4, 8, 8)]
    return pl.pallas_call(
        reduce_kernel,
        out_shape=jax.ShapeDtypeStruct((rows, width), F32),
        in_specs=[pl.BlockSpec(memory_space=pltpu.VMEM)],
        out_specs=pl.BlockSpec(memory_space=pltpu.VMEM),
        scratch_shapes=blocks
        + [pltpu.SemaphoreType.DMA((20,)), pltpu.SemaphoreType.DMA((20,))],
        compiler_params=pltpu.CompilerParams(
            collective_id=1, has_side_effects=True, vmem_limit_bytes=32 << 20
        ),
    )(value)


def per_device(
    tokens, norm_gain, gate_weights, exit_flags, routes, next_device, up_weight, down_weight
):
    row_count, width = tokens.shape
    owners = lax.axis_size("expert")
    reps = lax.axis_size("rep")
    local_experts = up_weight.shape[0]
    top = routes.shape[1]
    experts_all = local_experts * owners
    most_live = row_count // 2
    cap = top * most_live // experts_all
    hand_cap = (most_live + owners - 1) // owners
    packed_rows = owners * hand_cap

    live = exit_flags == 0
    dest_hot = (
        (next_device[:, None] == jnp.arange(owners)[None, :]) & live[:, None]
    ).astype(BF16)
    before = jnp.dot(lower_ones(row_count), dest_hot, preferred_element_type=F32)
    pos = jnp.sum(before * dest_hot.astype(F32), axis=1).astype(jnp.int32)
    slot = jnp.where(live, next_device * hand_cap + pos, packed_rows)
    pick = slot[None, :] == jnp.arange(packed_rows)[:, None]
    packed = jnp.dot(pick.astype(BF16), tokens, preferred_element_type=F32)
    square = jnp.sum(packed * packed, axis=1)
    dense_gate = jnp.sum(
        jnp.where(
            routes[:, :, None] == jnp.arange(experts_all)[None, None, :],
            gate_weights[:, :, None],
            0.0,
        ),
        axis=1,
    )
    gate_packed = jnp.sum(
        jnp.where(pick[:, :, None], dense_gate[None, :, :], 0.0), axis=1
    )
    aux = jnp.concatenate([gate_packed, square[:, None]], axis=1)

    pieces = []
    rest = aux
    for _ in range(3):
        piece = lax.reduce_precision(rest, 8, 7)
        pieces.append(piece.astype(BF16))
        rest = rest - piece
    side = jnp.concatenate(pieces, axis=1)
    side = jnp.pad(side, ((0, 0), (0, -side.shape[1] % 128)))
    both = expert_gather(jnp.concatenate([packed.astype(BF16), side], axis=1))
    rows = both[:, :, :width]
    parts = both[:, :, width : width + 3 * aux.shape[1]].astype(F32)
    parts = parts.reshape(owners, packed_rows, 3, aux.shape[1])
    aux = parts[:, :, 0] + parts[:, :, 1] + parts[:, :, 2]
    rinv = lax.rsqrt(lax.psum(aux[:, :, experts_all], "rep") / (width * reps) + 1e-06)

    me = lax.axis_index("expert")
    gates = lax.dynamic_slice_in_dim(aux, me * local_experts, local_experts, axis=2)
    routed = (gates > 0).astype(BF16)
    place = jnp.einsum(
        "rt,ite->ire", lower_ones(packed_rows), routed, preferred_element_type=F32
    ).astype(jnp.int32)
    hot = (place[:, :, :, None] == jnp.arange(cap)) & (routed > 0)[:, :, :, None]
    hot = hot.reshape(owners, packed_rows, local_experts * cap)
    slots = jnp.einsum("irs,ird->isd", hot.astype(BF16), rows, preferred_element_type=F32)
    rinv_slot = jnp.sum(jnp.where(hot, rinv[:, :, None], 0.0), axis=1)
    normed = (slots * rinv_slot[:, :, None] * norm_gain).astype(BF16)
    normed = normed.reshape(owners, local_experts, cap, width)

    outs = []
    sums = []
    for e in range(local_experts):
        flat = normed[:, e].reshape(owners * cap, width)
        sums.append(
            rep_sum(jnp.dot(flat, up_weight[e], preferred_element_type=F32), reps)
        )
    for e in range(local_experts):
        act = jax.nn.silu(sums[e]).astype(BF16)
        out = jnp.dot(act, down_weight[e], preferred_element_type=F32).astype(BF16)
        outs.append(out.reshape(owners, cap, width))
    out = jnp.stack(outs, axis=1)
    out = out.reshape(owners * local_experts * cap, width)

    gate_slot = jnp.where(hot, jnp.repeat(gates, cap, axis=2), 0.0).astype(BF16)
    gate_slot = gate_slot.reshape(owners, owners, hand_cap, -1).transpose(1, 0, 2, 3)
    same = jnp.arange(owners)[:, None] == jnp.arange(owners)[None, :]
    weights = jnp.where(same[None, :, None, :, None], gate_slot[:, :, :, None, :], 0)
    weights = weights.reshape(owners * packed_rows, -1)
    mix = jnp.dot(weights, out, preferred_element_type=F32).astype(BF16)
    summed = expert_reduce(mix.reshape(owners, packed_rows, width))
    own = lax.dynamic_slice_in_dim(
        rows.reshape(owners, owners, hand_cap, width), me, 1, axis=1
    )[:, 0]
    return own.reshape(packed_rows, width).astype(F32) + summed.astype(F32)


def solution(mesh):
    in_specs = (
        P("expert", "rep"),
        P("rep"),
        P("expert", None),
        P("expert"),
        P("expert", None),
        P("expert"),
        P("expert", "rep", None),
        P("expert", None, "rep"),
    )
    return jax.shard_map(
        per_device, mesh=mesh, in_specs=in_specs, out_specs=P("expert", "rep"), check_vma=False
    )
```

```python
import functools

import jax
import jax.numpy as jnp
from jax import lax
from jax.experimental import pallas as pl
from jax.experimental.pallas import tpu as pltpu
from jax.sharding import PartitionSpec as P

F32 = jnp.float32
BF16 = jnp.bfloat16


def lower_ones(n):
    i = jnp.arange(n)
    return (i[:, None] > i[None, :]).astype(BF16)


def rep_sum(value, reps, kind=BF16):
    if reps != 2:
        return lax.psum(value, "rep")
    return value + lax.ppermute(value.astype(kind), "rep", [(0, 1), (1, 0)]).astype(F32)


Z, X, C = 4, 2, 2
MESH = pl.DeviceIdType.MESH


def place_of():
    me = lax.axis_index("expert")
    return lax.axis_index("rep"), me // (X * C), me // C % X, me % C


def index_of(z, x, c):
    return (z * X + x) * C + c


def greet(rep, z, x, c):
    barrier = pltpu.get_barrier_semaphore()

    def signal(where):
        pl.semaphore_signal(barrier, inc=1, device_id=(rep, where), device_id_type=MESH)

    signal(index_of(z, 1 - x, c))
    signal(index_of(z, x, 1 - c))
    pl.when(z > 0)(lambda: signal(index_of(z - 1, x, c)))
    pl.when(z < Z - 1)(lambda: signal(index_of(z + 1, x, c)))
    inner = (z > 0) & (z < Z - 1)
    pl.when(inner)(lambda: pl.semaphore_wait(barrier, 4))
    pl.when(jnp.logical_not(inner))(lambda: pl.semaphore_wait(barrier, 3))


def gather_kernel(own, out, local_sem, send, recv):
    rep, z, x, c = place_of()
    mine = index_of(z, x, c)
    greet(rep, z, x, c)
    local = pltpu.make_async_copy(own, out.at[mine], local_sem)
    local.start()

    def copy(block, sem, where, source=None):
        return pltpu.make_async_remote_copy(
            src_ref=out.at[block] if source is None else source,
            dst_ref=out.at[block],
            send_sem=send.at[sem],
            recv_sem=recv.at[block],
            device_id=(rep, where),
            device_id_type=MESH,
        )

    def forward(act):
        for d in range(Z):
            for sign in (1, -1):
                if d == 0 and sign < 0:
                    continue
                src = z - sign * d
                ok = (src >= 0) & (src < Z)

                def step(d=d, sign=sign, src=src):
                    block = index_of(src, x, c)
                    source = own if d == 0 else None
                    if d > 0:
                        act.wait(copy(block, 0, mine))
                    if d == 0 or sign > 0:
                        pl.when(z < Z - 1)(
                            lambda: act(copy(block, d, index_of(z + 1, x, c), source))
                        )
                    if d == 0 or sign < 0:
                        pl.when(z > 0)(
                            lambda: act(copy(block, 4 + d, index_of(z - 1, x, c), source))
                        )
                    act(copy(block, 8 + src, index_of(z, 1 - x, c), source))
                    act(copy(block, 12 + src, index_of(z, x, 1 - c), source))

                if d == 0:
                    step()
                else:
                    pl.when(ok)(step)
        for d in range(Z):
            for sign in (1, -1):
                if d == 0 and sign < 0:
                    continue
                src = z - sign * d

                def step(src=src):
                    block = index_of(src, 1 - x, c)
                    act.wait(copy(block, 0, mine))
                    act(copy(block, 16 + src, index_of(z, x, 1 - c)))

                pl.when((src >= 0) & (src < Z))(step)

    class Start:
        def __call__(self, op):
            op.start()

        def wait(self, op):
            op.wait_recv()

    class Finish:
        def __call__(self, op):
            op.wait_send()

        def wait(self, op):
            pass

    forward(Start())
    for a in range(Z):
        for b in range(X):
            copy(index_of(a, b, 1 - c), 0, mine).wait_recv()
    forward(Finish())
    local.wait()


def expert_gather(value):
    if (lax.axis_size("rep"), lax.axis_size("expert")) != (2, Z * X * C):
        return lax.all_gather(value, "expert")
    n = Z * X * C
    return pl.pallas_call(
        gather_kernel,
        out_shape=jax.ShapeDtypeStruct((n,) + value.shape, value.dtype),
        in_specs=[pl.BlockSpec(memory_space=pltpu.VMEM)],
        out_specs=pl.BlockSpec(memory_space=pltpu.VMEM),
        scratch_shapes=[
            pltpu.SemaphoreType.DMA,
            pltpu.SemaphoreType.DMA((20,)),
            pltpu.SemaphoreType.DMA((n,)),
        ],
        compiler_params=pltpu.CompilerParams(
            collective_id=0, has_side_effects=True, vmem_limit_bytes=24 << 20
        ),
    )(value)


def reduce_kernel(value, out, acc, from_c, from_x, part, from_z, send, recv):
    rep, z, x, c = place_of()
    greet(rep, z, x, c)

    def copy(source, target, sem, z2, x2, c2):
        return pltpu.make_async_remote_copy(
            src_ref=source,
            dst_ref=target,
            send_sem=send.at[sem],
            recv_sem=recv.at[sem],
            device_id=(rep, index_of(z2, x2, c2)),
            device_id_type=MESH,
        )

    order = (Z - 1, 0, 1, 2)

    def to_c(a, far):
        b = 1 - x if far else x
        k = (0 if far else Z) + a
        return copy(value.at[index_of(a, b, 1 - c)], from_c.at[k], k, z, x, 1 - c)

    def to_x(a):
        return copy(acc.at[a], from_x.at[a], 8 + a, z, 1 - x, c)

    def to_z(a, way):
        k = way * Z + a
        return copy(part.at[k], from_z.at[k], 12 + k, z + 1 - 2 * way, x, c)

    def arrived(a, way):
        k = way * Z + a
        copy(part.at[k], from_z.at[k], 12 + k, z, x, 1 - c).wait_recv()

    def wide(ref):
        return ref.astype(F32)

    for far in (True, False):
        for a in order:
            to_c(a, far).start()
    for a in order:
        to_c(a, True).wait_recv()
        acc[a] = (wide(value[index_of(a, 1 - x, c)]) + wide(from_c[a])).astype(BF16)
        to_x(a).start()
    for a in order:
        to_c(a, False).wait_recv()
        acc[Z + a] = (wide(value[index_of(a, x, c)]) + wide(from_c[Z + a])).astype(BF16)
    def on(way, a):
        k = way * Z + a
        arrived(a, way)
        part[k] = (wide(acc[Z + a]) + wide(from_z[k])).astype(BF16)
        to_z(a, way).start()

    for a in order:
        to_x(a).wait_recv()
        acc[Z + a] = (wide(acc[Z + a]) + wide(from_x[a])).astype(BF16)

        def first(way, a=a):
            part[way * Z + a] = acc[Z + a]
            to_z(a, way).start()

        pl.when((z == 0) & (a > z))(functools.partial(first, 0))
        pl.when((z == Z - 1) & (a < z))(functools.partial(first, 1))
        pl.when((z > 0) & (a > z))(functools.partial(on, 0, a))
        pl.when((z < Z - 1) & (a < z))(functools.partial(on, 1, a))

    out[...] = wide(acc[Z + z])

    def last(way):
        arrived(z, way)
        out[...] += wide(from_z[way * Z + z])

    pl.when(z > 0)(functools.partial(last, 0))
    pl.when(z < Z - 1)(functools.partial(last, 1))
    for a in range(Z):
        to_c(a, True).wait_send()
        to_c(a, False).wait_send()
        to_x(a).wait_send()
        pl.when(a > z)(lambda a=a: to_z(a, 0).wait_send())
        pl.when(a < z)(lambda a=a: to_z(a, 1).wait_send())


def expert_reduce(value):
    n, rows, width = value.shape
    if (lax.axis_size("rep"), n) != (2, Z * X * C):
        return lax.psum_scatter(value, "expert", scatter_dimension=0, tiled=False)
    blocks = [pltpu.VMEM((k, rows, width), BF16) for k in (8, 8, 4, 8, 8)]
    return pl.pallas_call(
        reduce_kernel,
        out_shape=jax.ShapeDtypeStruct((rows, width), F32),
        in_specs=[pl.BlockSpec(memory_space=pltpu.VMEM)],
        out_specs=pl.BlockSpec(memory_space=pltpu.VMEM),
        scratch_shapes=blocks
        + [pltpu.SemaphoreType.DMA((20,)), pltpu.SemaphoreType.DMA((20,))],
        compiler_params=pltpu.CompilerParams(
            collective_id=1, has_side_effects=True, vmem_limit_bytes=32 << 20
        ),
    )(value)


def per_device(
    tokens, norm_gain, gate_weights, exit_flags, routes, next_device, up_weight, down_weight
):
    row_count, width = tokens.shape
    owners = lax.axis_size("expert")
    reps = lax.axis_size("rep")
    local_experts = up_weight.shape[0]
    top = routes.shape[1]
    experts_all = local_experts * owners
    most_live = row_count // 2
    cap = top * most_live // experts_all
    hand_cap = (most_live + owners - 1) // owners
    packed_rows = owners * hand_cap

    live = exit_flags == 0
    dest_hot = (
        (next_device[:, None] == jnp.arange(owners)[None, :]) & live[:, None]
    ).astype(BF16)
    before = jnp.dot(lower_ones(row_count), dest_hot, preferred_element_type=F32)
    pos = jnp.sum(before * dest_hot.astype(F32), axis=1).astype(jnp.int32)
    slot = jnp.where(live, next_device * hand_cap + pos, packed_rows)
    pick = slot[None, :] == jnp.arange(packed_rows)[:, None]
    packed = jnp.dot(pick.astype(BF16), tokens, preferred_element_type=F32)
    square = jnp.sum(packed * packed, axis=1)
    dense_gate = jnp.sum(
        jnp.where(
            routes[:, :, None] == jnp.arange(experts_all)[None, None, :],
            gate_weights[:, :, None],
            0.0,
        ),
        axis=1,
    )
    gate_packed = jnp.sum(
        jnp.where(pick[:, :, None], dense_gate[None, :, :], 0.0), axis=1
    )
    aux = jnp.concatenate([gate_packed, square[:, None]], axis=1)

    pieces = []
    rest = aux
    for _ in range(3):
        piece = lax.reduce_precision(rest, 8, 7)
        pieces.append(piece.astype(BF16))
        rest = rest - piece
    side = jnp.concatenate(pieces, axis=1)
    side = jnp.pad(side, ((0, 0), (0, -side.shape[1] % 128)))
    both = expert_gather(jnp.concatenate([packed.astype(BF16), side], axis=1))
    parts = both[:, :, width : width + 3 * aux.shape[1]].astype(F32)
    parts = parts.reshape(owners, packed_rows, 3, aux.shape[1])
    aux = parts[:, :, 0] + parts[:, :, 1] + parts[:, :, 2]
    rinv = lax.rsqrt(rep_sum(aux[:, :, experts_all], reps, F32) / (width * reps) + 1e-06)

    me = lax.axis_index("expert")
    gates = lax.dynamic_slice_in_dim(aux, me * local_experts, local_experts, axis=2)
    routed = (gates > 0).astype(BF16)
    place = jnp.einsum(
        "rt,ite->ire", lower_ones(packed_rows), routed, preferred_element_type=F32
    ).astype(jnp.int32)
    hot = (place[:, :, :, None] == jnp.arange(cap)) & (routed > 0)[:, :, :, None]
    hot = hot.reshape(owners, packed_rows, local_experts * cap)
    slots = jnp.einsum("irs,ird->isd", hot.astype(BF16), both, preferred_element_type=F32)[
        :, :, :width
    ]
    rinv_slot = jnp.sum(jnp.where(hot, rinv[:, :, None], 0.0), axis=1)
    normed = (slots * rinv_slot[:, :, None] * norm_gain).astype(BF16)
    normed = normed.reshape(owners, local_experts, cap, width)

    outs = []
    sums = []
    for e in range(local_experts):
        flat = normed[:, e].reshape(owners * cap, width)
        sums.append(
            rep_sum(jnp.dot(flat, up_weight[e], preferred_element_type=F32), reps)
        )
    for e in range(local_experts):
        act = jax.nn.silu(sums[e]).astype(BF16)
        out = jnp.dot(act, down_weight[e], preferred_element_type=F32).astype(BF16)
        outs.append(out.reshape(owners, cap, width))
    out = jnp.stack(outs, axis=1)
    out = out.reshape(owners * local_experts * cap, width)

    gate_slot = jnp.where(hot, jnp.repeat(gates, cap, axis=2), 0.0).astype(BF16)
    gate_slot = gate_slot.reshape(owners, owners, hand_cap, -1).transpose(1, 0, 2, 3)
    count = local_experts * cap
    gate_slot = gate_slot.reshape(owners * packed_rows, count)
    column = jnp.arange(owners * count)
    spread = (jnp.arange(count)[:, None] == column[None, :] % count).astype(BF16)
    block = jnp.arange(owners * packed_rows) // hand_cap % owners
    weights = jnp.dot(gate_slot, spread, preferred_element_type=F32)
    weights = jnp.where(block[:, None] == column[None, :] // count, weights, 0.0).astype(BF16)
    mix = jnp.dot(weights, out, preferred_element_type=F32).astype(BF16)
    summed = expert_reduce(mix.reshape(owners, packed_rows, width))
    own = lax.dynamic_slice_in_dim(both, me * hand_cap, hand_cap, axis=1)[:, :, :width]
    return own.reshape(packed_rows, width).astype(F32) + summed.astype(F32)


def solution(mesh):
    in_specs = (
        P("expert", "rep"),
        P("rep"),
        P("expert", None),
        P("expert"),
        P("expert", None),
        P("expert"),
        P("expert", "rep", None),
        P("expert", None, "rep"),
    )
    return jax.shard_map(
        per_device, mesh=mesh, in_specs=in_specs, out_specs=P("expert", "rep"), check_vma=False
    )
```

```python
import functools

import jax
import jax.numpy as jnp
from jax import lax
from jax.experimental import pallas as pl
from jax.experimental.pallas import tpu as pltpu
from jax.sharding import PartitionSpec as P

F32 = jnp.float32
BF16 = jnp.bfloat16


def lower_ones(n):
    i = jnp.arange(n)
    return (i[:, None] > i[None, :]).astype(BF16)


def rep_sum(value, reps, kind=BF16):
    if reps != 2:
        return lax.psum(value, "rep")
    return value + lax.ppermute(value.astype(kind), "rep", [(0, 1), (1, 0)]).astype(F32)


Z, X, C = 4, 2, 2
MESH = pl.DeviceIdType.MESH


def place_of():
    me = lax.axis_index("expert")
    return lax.axis_index("rep"), me // (X * C), me // C % X, me % C


def index_of(z, x, c):
    return (z * X + x) * C + c


def greet(rep, z, x, c):
    barrier = pltpu.get_barrier_semaphore()

    def signal(where):
        pl.semaphore_signal(barrier, inc=1, device_id=(rep, where), device_id_type=MESH)

    signal(index_of(z, 1 - x, c))
    signal(index_of(z, x, 1 - c))
    pl.when(z > 0)(lambda: signal(index_of(z - 1, x, c)))
    pl.when(z < Z - 1)(lambda: signal(index_of(z + 1, x, c)))
    inner = (z > 0) & (z < Z - 1)
    pl.when(inner)(lambda: pl.semaphore_wait(barrier, 4))
    pl.when(jnp.logical_not(inner))(lambda: pl.semaphore_wait(barrier, 3))


def gather_kernel(own, out, local_sem, send, recv):
    rep, z, x, c = place_of()
    mine = index_of(z, x, c)
    greet(rep, z, x, c)
    local = pltpu.make_async_copy(own, out.at[mine], local_sem)
    local.start()

    def copy(block, sem, where, source=None):
        return pltpu.make_async_remote_copy(
            src_ref=out.at[block] if source is None else source,
            dst_ref=out.at[block],
            send_sem=send.at[sem],
            recv_sem=recv.at[block],
            device_id=(rep, where),
            device_id_type=MESH,
        )

    def forward(act):
        for d in range(Z):
            for sign in (1, -1):
                if d == 0 and sign < 0:
                    continue
                src = z - sign * d
                ok = (src >= 0) & (src < Z)

                def step(d=d, sign=sign, src=src):
                    block = index_of(src, x, c)
                    source = own if d == 0 else None
                    if d > 0:
                        act.wait(copy(block, 0, mine))
                    if d == 0 or sign > 0:
                        pl.when(z < Z - 1)(
                            lambda: act(copy(block, d, index_of(z + 1, x, c), source))
                        )
                    if d == 0 or sign < 0:
                        pl.when(z > 0)(
                            lambda: act(copy(block, 4 + d, index_of(z - 1, x, c), source))
                        )
                    act(copy(block, 8 + src, index_of(z, 1 - x, c), source))
                    act(copy(block, 12 + src, index_of(z, x, 1 - c), source))

                if d == 0:
                    step()
                else:
                    pl.when(ok)(step)
        for d in range(Z):
            for sign in (1, -1):
                if d == 0 and sign < 0:
                    continue
                src = z - sign * d

                def step(src=src):
                    block = index_of(src, 1 - x, c)
                    act.wait(copy(block, 0, mine))
                    act(copy(block, 16 + src, index_of(z, x, 1 - c)))

                pl.when((src >= 0) & (src < Z))(step)

    class Start:
        def __call__(self, op):
            op.start()

        def wait(self, op):
            op.wait_recv()

    class Finish:
        def __call__(self, op):
            op.wait_send()

        def wait(self, op):
            pass

    forward(Start())
    for a in range(Z):
        for b in range(X):
            copy(index_of(a, b, 1 - c), 0, mine).wait_recv()
    forward(Finish())
    local.wait()


def expert_gather(value):
    if (lax.axis_size("rep"), lax.axis_size("expert")) != (2, Z * X * C):
        return lax.all_gather(value, "expert")
    n = Z * X * C
    return pl.pallas_call(
        gather_kernel,
        out_shape=jax.ShapeDtypeStruct((n,) + value.shape, value.dtype),
        in_specs=[pl.BlockSpec(memory_space=pltpu.VMEM)],
        out_specs=pl.BlockSpec(memory_space=pltpu.VMEM),
        scratch_shapes=[
            pltpu.SemaphoreType.DMA,
            pltpu.SemaphoreType.DMA((20,)),
            pltpu.SemaphoreType.DMA((n,)),
        ],
        compiler_params=pltpu.CompilerParams(
            collective_id=0, has_side_effects=True, vmem_limit_bytes=24 << 20
        ),
    )(value)


def reduce_kernel(value, out, acc, from_c, from_x, part, from_z, send, recv):
    rep, z, x, c = place_of()
    greet(rep, z, x, c)

    def copy(source, target, sem, z2, x2, c2):
        return pltpu.make_async_remote_copy(
            src_ref=source,
            dst_ref=target,
            send_sem=send.at[sem],
            recv_sem=recv.at[sem],
            device_id=(rep, index_of(z2, x2, c2)),
            device_id_type=MESH,
        )

    order = (Z - 1, 0, 1, 2)

    def to_c(a, far):
        b = 1 - x if far else x
        k = (0 if far else Z) + a
        return copy(value.at[index_of(a, b, 1 - c)], from_c.at[k], k, z, x, 1 - c)

    def to_x(a):
        return copy(acc.at[a], from_x.at[a], 8 + a, z, 1 - x, c)

    def to_z(a, way):
        k = way * Z + a
        return copy(part.at[k], from_z.at[k], 12 + k, z + 1 - 2 * way, x, c)

    def arrived(a, way):
        k = way * Z + a
        copy(part.at[k], from_z.at[k], 12 + k, z, x, 1 - c).wait_recv()

    def wide(ref):
        return ref.astype(F32)

    for far in (True, False):
        for a in order:
            to_c(a, far).start()
    for a in order:
        to_c(a, True).wait_recv()
        acc[a] = (wide(value[index_of(a, 1 - x, c)]) + wide(from_c[a])).astype(BF16)
        to_x(a).start()
    for a in order:
        to_c(a, False).wait_recv()
        acc[Z + a] = (wide(value[index_of(a, x, c)]) + wide(from_c[Z + a])).astype(BF16)
    def on(way, a):
        k = way * Z + a
        arrived(a, way)
        part[k] = (wide(acc[Z + a]) + wide(from_z[k])).astype(BF16)
        to_z(a, way).start()

    for a in order:
        to_x(a).wait_recv()
        acc[Z + a] = (wide(acc[Z + a]) + wide(from_x[a])).astype(BF16)

        def first(way, a=a):
            part[way * Z + a] = acc[Z + a]
            to_z(a, way).start()

        pl.when((z == 0) & (a > z))(functools.partial(first, 0))
        pl.when((z == Z - 1) & (a < z))(functools.partial(first, 1))
        pl.when((z > 0) & (a > z))(functools.partial(on, 0, a))
        pl.when((z < Z - 1) & (a < z))(functools.partial(on, 1, a))

    out[...] = wide(acc[Z + z])

    def last(way):
        arrived(z, way)
        out[...] += wide(from_z[way * Z + z])

    pl.when(z > 0)(functools.partial(last, 0))
    pl.when(z < Z - 1)(functools.partial(last, 1))
    for a in range(Z):
        to_c(a, True).wait_send()
        to_c(a, False).wait_send()
        to_x(a).wait_send()
        pl.when(a > z)(lambda a=a: to_z(a, 0).wait_send())
        pl.when(a < z)(lambda a=a: to_z(a, 1).wait_send())


def expert_reduce(value):
    n, rows, width = value.shape
    if (lax.axis_size("rep"), n) != (2, Z * X * C):
        return lax.psum_scatter(value, "expert", scatter_dimension=0, tiled=False)
    blocks = [pltpu.VMEM((k, rows, width), BF16) for k in (8, 8, 4, 8, 8)]
    return pl.pallas_call(
        reduce_kernel,
        out_shape=jax.ShapeDtypeStruct((rows, width), F32),
        in_specs=[pl.BlockSpec(memory_space=pltpu.VMEM)],
        out_specs=pl.BlockSpec(memory_space=pltpu.VMEM),
        scratch_shapes=blocks
        + [pltpu.SemaphoreType.DMA((20,)), pltpu.SemaphoreType.DMA((20,))],
        compiler_params=pltpu.CompilerParams(
            collective_id=1, has_side_effects=True, vmem_limit_bytes=32 << 20
        ),
    )(value)


def per_device(
    tokens, norm_gain, gate_weights, exit_flags, routes, next_device, up_weight, down_weight
):
    row_count, width = tokens.shape
    owners = lax.axis_size("expert")
    reps = lax.axis_size("rep")
    local_experts = up_weight.shape[0]
    top = routes.shape[1]
    experts_all = local_experts * owners
    most_live = row_count // 2
    cap = top * most_live // experts_all
    hand_cap = (most_live + owners - 1) // owners
    packed_rows = owners * hand_cap

    live = exit_flags == 0
    dest_hot = (
        (next_device[:, None] == jnp.arange(owners)[None, :]) & live[:, None]
    ).astype(BF16)
    before = jnp.dot(lower_ones(row_count), dest_hot, preferred_element_type=F32)
    pos = jnp.sum(before * dest_hot.astype(F32), axis=1).astype(jnp.int32)
    slot = jnp.where(live, next_device * hand_cap + pos, packed_rows)
    pick = slot[None, :] == jnp.arange(packed_rows)[:, None]
    packed = jnp.dot(pick.astype(BF16), tokens, preferred_element_type=F32)
    square = jnp.sum(packed * packed, axis=1)
    dense_gate = jnp.sum(
        jnp.where(
            routes[:, :, None] == jnp.arange(experts_all)[None, None, :],
            gate_weights[:, :, None],
            0.0,
        ),
        axis=1,
    )
    gate_packed = jnp.sum(
        jnp.where(pick[:, :, None], dense_gate[None, :, :], 0.0), axis=1
    )
    aux = jnp.concatenate([gate_packed, square[:, None]], axis=1)

    pieces = []
    rest = aux
    for _ in range(3):
        piece = lax.reduce_precision(rest, 8, 7)
        pieces.append(piece.astype(BF16))
        rest = rest - piece
    side = jnp.concatenate(pieces, axis=1)
    side = jnp.pad(side, ((0, 0), (0, -side.shape[1] % 128)))
    both = expert_gather(jnp.concatenate([packed.astype(BF16), side], axis=1))
    parts = both[:, :, width : width + 3 * aux.shape[1]].astype(F32)
    parts = parts.reshape(owners, packed_rows, 3, aux.shape[1])
    aux = parts[:, :, 0] + parts[:, :, 1] + parts[:, :, 2]
    rinv = lax.rsqrt(rep_sum(aux[:, :, experts_all], reps, F32) / (width * reps) + 1e-06)

    me = lax.axis_index("expert")
    gates = lax.dynamic_slice_in_dim(aux, me * local_experts, local_experts, axis=2)
    routed = (gates > 0).astype(BF16)
    place = jnp.einsum(
        "rt,ite->ire", lower_ones(packed_rows), routed, preferred_element_type=F32
    ).astype(jnp.int32)
    hot = (place[:, :, :, None] == jnp.arange(cap)) & (routed > 0)[:, :, :, None]
    hot = hot.reshape(owners, packed_rows, local_experts * cap)
    slots = jnp.einsum("irs,ird->isd", hot.astype(BF16), both, preferred_element_type=F32)[
        :, :, :width
    ]
    rinv_slot = jnp.sum(jnp.where(hot, rinv[:, :, None], 0.0), axis=1)
    normed = (slots * rinv_slot[:, :, None] * norm_gain).astype(BF16)
    normed = normed.reshape(owners, local_experts, cap, width)

    outs = []
    sums = []
    for e in range(local_experts):
        flat = normed[:, e].reshape(owners * cap, width)
        halves = [
            rep_sum(jnp.dot(flat, part, preferred_element_type=F32), reps)
            for part in jnp.split(up_weight[e], 2, axis=1)
        ]
        sums.append(jnp.concatenate(halves, axis=1))
    for e in range(local_experts):
        act = jax.nn.silu(sums[e]).astype(BF16)
        out = jnp.dot(act, down_weight[e], preferred_element_type=F32).astype(BF16)
        outs.append(out.reshape(owners, cap, width))
    out = jnp.stack(outs, axis=1)
    out = out.reshape(owners * local_experts * cap, width)

    gate_slot = jnp.where(hot, jnp.repeat(gates, cap, axis=2), 0.0).astype(BF16)
    gate_slot = gate_slot.reshape(owners, owners, hand_cap, -1).transpose(1, 0, 2, 3)
    count = local_experts * cap
    gate_slot = gate_slot.reshape(owners * packed_rows, count)
    column = jnp.arange(owners * count)
    spread = (jnp.arange(count)[:, None] == column[None, :] % count).astype(BF16)
    block = jnp.arange(owners * packed_rows) // hand_cap % owners
    weights = jnp.dot(gate_slot, spread, preferred_element_type=F32)
    weights = jnp.where(block[:, None] == column[None, :] // count, weights, 0.0).astype(BF16)
    mix = jnp.dot(weights, out, preferred_element_type=F32).astype(BF16)
    summed = expert_reduce(mix.reshape(owners, packed_rows, width))
    own = lax.dynamic_slice_in_dim(both, me * hand_cap, hand_cap, axis=1)[:, :, :width]
    return own.reshape(packed_rows, width).astype(F32) + summed.astype(F32)


def solution(mesh):
    in_specs = (
        P("expert", "rep"),
        P("rep"),
        P("expert", None),
        P("expert"),
        P("expert", None),
        P("expert"),
        P("expert", "rep", None),
        P("expert", None, "rep"),
    )
    return jax.shard_map(
        per_device, mesh=mesh, in_specs=in_specs, out_specs=P("expert", "rep"), check_vma=False
    )
```
